32 devices in a mesh: island: 4 (over y, x), fsdp: 8 (over z, core).
Axes of the slice: x: 2, y: 2, z: 4, core: 2. Of those that a mesh axis runs over, the one named last changes fastest.
Arguments:
- tokens: bfloat16 [8192, 4096], P(('island', 'fsdp')), may hold values from -6 to 6
- upstream: bfloat16 [8192, 1024], P(('island', 'fsdp')), may hold values from -6 to 6
- params: float32 [4096, 1024], P('fsdp'), may hold values from -6 to 6
- momentum: float32 [4096, 1024], P('fsdp'), may hold values from -4 to 4
- projection: float32 [1024, 512], replicated, may hold values from -6 to 6
Outputs:
- values: bfloat16 [8192, 1024], P(('island', 'fsdp'))
- token_grads: bfloat16 [8192, 4096], P(('island', 'fsdp'))
- new_params: float32 [4096, 1024], P('fsdp')
- new_momentum: float32 [4096, 1024], P('fsdp')
The draws below stay inside these ranges and needn't reach their ends.
All inputs are finite; a program needn't handle non-finite values.
Results may differ from the reference program's by a relative error of at most 0.012.
Values may be sent and summed in bfloat16 or wider, within the bound.
A program may use at most 128 MiB of HBM per device.

```python
import math
import jax
import jax.numpy as jnp
from jax import lax

D = 4096
KV = 1024
PROJ = 512
TOK_ISL = 2048
TOK_ALL = 8192
N_ISLAND = 4


def steps_of(stream_key, dims, cuts, least, largest):
    gain, own = 1.0, jax.random.fold_in(stream_key, 6)
    for position, parts in cuts:
        heights = jnp.exp(jax.random.uniform(jax.random.fold_in(own, position), (parts,), jnp.float32, least / len(cuts), largest / len(cuts)))
        gain = gain * jnp.repeat(heights, dims[position] // parts).reshape([-1 if axis == position else 1 for axis in range(len(dims))])
    return gain


def gaussian(key, shape, width, reach, cuts=(), dtype=jnp.bfloat16):
    entries = jax.random.normal(key, shape, jnp.float32) * width
    if len(cuts) > 0:
        entries = steps_of(key, shape, cuts, -0.22, 0.18) * entries
    return jnp.clip(entries, min=-reach, max=reach).astype(dtype)


def setup_inputs(seed: int = 0) -> dict:
    seeds = jax.random.split(jax.random.key(seed), 6)
    tokens = gaussian(seeds[0], (TOK_ALL, D), 1.0, 6.0, ((0, 32),))
    upstream = gaussian(seeds[1], (TOK_ALL, KV), 1.0, 6.0, ((0, 32),))
    params = gaussian(seeds[2], (D, KV), 1.0, 6.0, ((0, 8),), jnp.float32)
    momentum = gaussian(seeds[3], (D, KV), 0.5, 4.0, ((0, 8),), jnp.float32)
    projection = gaussian(seeds[4], (KV, PROJ), 1.0, 6.0, (), jnp.float32)
    return dict(tokens=tokens, upstream=upstream, params=params, momentum=momentum, projection=projection)


def reference(tokens, upstream, params, momentum, projection):
    half_weight = params.astype(jnp.bfloat16)
    inv_width = 1.0 / math.sqrt(D)
    forward_sum = jnp.dot(tokens, half_weight, preferred_element_type=jnp.float32)
    values = (forward_sum * inv_width).astype(jnp.bfloat16)
    backward_sum = lax.dot_general(upstream, half_weight, (((1,), (1,)), ((), ())), preferred_element_type=jnp.float32)
    token_grads = (backward_sum * inv_width).astype(jnp.bfloat16)
    summed = lax.dot_general(tokens, upstream, (((0,), (0,)), ((), ())), preferred_element_type=jnp.float32)
    pseudo = summed * (1.0 / math.sqrt(TOK_ISL))
    compressed = jnp.dot(pseudo, projection, precision=lax.Precision.HIGHEST)
    outer = jnp.dot(compressed, projection.T, precision=lax.Precision.HIGHEST) / (PROJ * N_ISLAND)
    new_momentum = 0.9 * momentum + outer
    new_params = params - 0.7 * (outer + 0.9 * new_momentum)
    return (values, token_grads, new_params, new_momentum)
```

```python
import functools
import math

import jax
import jax.numpy as jnp
from jax import lax
from jax.experimental import pallas as pl
from jax.experimental.pallas import tpu as pltpu
from jax.sharding import PartitionSpec as P

MESH = pl.DeviceIdType.MESH
F32 = jnp.float32
BF16 = jnp.bfloat16


def kernel(Z, I, tok_h, up_h, par_h, mom_h, proj_h, val_h, tg_h, np_h, nm_h,
           tok, up, par, mom, proj, projb, w, s, gsend, grecv, h, pb, zb, zr, fin, acc, val, tg, nm,
           in_sem, out_sem, tg_sem, np_sem, nm_sem,
           own_s, own_r, ag_s, ag_r, pl_s, pl_r, sib_s, sib_r, g_s, g_r, rp_s, rp_r, rz_s, rz_r, f_s, f_r):
    i = lax.axis_index("island")
    f = lax.axis_index("fsdp")
    z, c = f // 2, f % 2
    o = 1 - c
    sib = (i, z * 2 + o)
    R, KV = w.shape[1] * w.shape[2], w.shape[3]
    inv_width = 1.0 / math.sqrt(tok.shape[1])

    def zto(d):
        return lax.rem(z + d, Z)

    def zfrom(d):
        return lax.rem(z - d + Z, Z)

    def ito(e):
        return lax.rem(i + e, I)

    def ifrom(e):
        return lax.rem(i - e + I, I)

    ins = [pltpu.make_async_copy(a, b, in_sem.at[k]) for k, (a, b) in enumerate(
        ((par_h, par), (up_h, up), (proj_h, proj), (tok_h, tok), (mom_h, mom)))]
    for cp in ins:
        cp.start()

    barrier = pltpu.get_barrier_semaphore()
    for d in range(1, Z):
        pl.semaphore_signal(barrier, inc=1, device_id=(i, zto(d) * 2 + c), device_id_type=MESH)
    for e in range(1, I):
        pl.semaphore_signal(barrier, inc=1, device_id=(ito(e), f), device_id_type=MESH)
    pl.semaphore_signal(barrier, inc=1, device_id=sib, device_id_type=MESH)

    def remote(src, dst, ss, rs, to):
        return pltpu.make_async_remote_copy(src_ref=src, dst_ref=dst, send_sem=ss, recv_sem=rs, device_id=to, device_id_type=MESH)

    def c_own(fb):
        return remote(w.at[fb], w.at[fb], own_s, own_r, sib)

    def c_ag(d, fb, part):
        return remote(w.at[fb, part], w.at[fb, part], ag_s.at[d], ag_r.at[d], (i, zto(d) * 2 + c))

    def c_plane(e, d, fb, part):
        return remote(w.at[fb, part], w.at[fb, part], pl_s.at[e, d], pl_r.at[e, d], (ito(e), f))

    def c_sib(e, d, fb, part):
        return remote(w.at[fb, part], w.at[fb, part], sib_s.at[e, d], sib_r.at[e, d], sib)

    def c_g(d):
        return remote(gsend.at[d], grecv.at[d], g_s.at[d], g_r.at[d], sib)

    def c_rp(e, d):
        return remote(h.at[d, ito(e)], pb.at[e, d], rp_s.at[e, d], rp_r.at[e, d], (ito(e), f))

    def c_rz(d):
        return remote(zb.at[d], zr.at[d], rz_s.at[d], rz_r.at[d], (i, zto(d) * 2 + c))

    def c_fin(e, part):
        return remote(fin.at[part], fin.at[part], f_s.at[e], f_r.at[e], (ito(e), f))

    ins[0].wait()
    w[f] = par[...].astype(BF16)
    pl.semaphore_wait(barrier, Z + I - 1)
    for d in range(1, Z):
        c_ag(d, f, i).start()
    c_own(f).start()

    ins[1].wait()
    ins[2].wait()
    projb[...] = proj[...].astype(BF16)
    s[...] = jnp.dot(up[...], projb[...], preferred_element_type=F32).astype(BF16)
    ins[3].wait()

    def cols(fb):
        return pl.ds(pl.multiple_of(fb * R, R), R)

    def gblock(fb):
        return lax.dot_general(tok[:, cols(fb)], s[...], (((0,), (0,)), ((), ())), preferred_element_type=F32)

    def send_g(d, carry):
        gsend[d] = gblock(zto(d) * 2 + o).astype(BF16)
        c_g(d).start()
        return carry

    lax.fori_loop(0, Z, send_g, 0)

    def send_rp(d, carry):
        mine = gblock(zto(d) * 2 + c)
        c_g(d).wait_recv()
        h[d] = (mine + grecv[d].astype(F32)).astype(BF16).reshape(h.shape[1:])
        for e in range(1, I):
            c_rp(e, d).start()
        return carry

    lax.fori_loop(0, Z, send_rp, 0)

    acc[...] = jnp.zeros_like(acc)

    def c_tg(fb):
        return pltpu.make_async_copy(tg.at[fb], tg_h.at[:, cols(fb)], tg_sem.at[fb])

    def block(fb):
        wb = w[fb].reshape(R, KV)
        acc[...] += jnp.dot(tok[:, cols(fb)], wb, preferred_element_type=F32)
        product = lax.dot_general(up[...], wb, (((1,), (1,)), ((), ())), preferred_element_type=F32)
        tg[fb] = (product * inv_width).astype(BF16)
        c_tg(fb).start()

    def forward(d, carry):
        fb = zfrom(d) * 2 + c
        c_ag(d, fb, i).wait_recv()
        for e in range(1, I):
            c_plane(e, d, fb, i).start()
        c_sib(0, d, fb, i).start()
        return carry

    lax.fori_loop(1, Z, forward, 0)

    def send_rz(d, carry):
        total = h[d, i].astype(F32)
        for e in range(1, I):
            c_rp(e, d).wait_recv()
            total += pb[e, d].astype(F32)
        zb[d] = total.astype(BF16)

        @pl.when(d > 0)
        def _():
            c_rz(d).start()

        return carry

    lax.fori_loop(0, Z, send_rz, 0)

    block(f)
    c_own(z * 2 + o).wait_recv()
    block(z * 2 + o)

    total = zb[0].astype(F32)
    for d in range(1, Z):
        c_rz(d).wait_recv()
        total += zr[d].astype(F32)
    fin[i] = total.astype(BF16)
    for e in range(1, I):
        c_fin(e, i).start()

    factor = 1.0 / (math.sqrt(tok.shape[0] * 2 * Z) * projb.shape[1] * I)
    ins[4].wait()

    def out_np(part):
        return pltpu.make_async_copy(par.at[part], np_h.at[part], np_sem.at[part])

    def out_nm(part):
        return pltpu.make_async_copy(nm.at[part], nm_h.at[part], nm_sem.at[part])

    def finish(e, carry):
        part = ifrom(e)

        @pl.when(e > 0)
        def _():
            c_fin(e, part).wait_recv()

        outer = lax.dot_general(fin[part], projb[...], (((1,), (1,)), ((), ())), preferred_element_type=F32) * factor
        new_momentum = 0.9 * mom[part] + outer
        nm[part] = new_momentum
        par[part] = par[part] - 0.7 * (outer + 0.9 * new_momentum)
        out_np(part).start()
        out_nm(part).start()
        return carry

    def take(d, carry):
        fb = zfrom(d) * 2 + c
        for e in range(1, I):
            part = ifrom(e)
            c_plane(e, d, fb, part).wait_recv()
            c_sib(e, d, fb, part).start()
        block(fb)
        fo = zfrom(d) * 2 + o
        for e in range(I):
            c_sib(e, d, fo, ifrom(e)).wait_recv()
        block(fo)
        return carry

    lax.fori_loop(1, Z, take, 0)
    val[...] = (acc[...] * inv_width).astype(BF16)
    out_val = pltpu.make_async_copy(val, val_h, out_sem)
    out_val.start()
    lax.fori_loop(0, I, finish, 0)

    def drain_z(d, carry):
        fb = zfrom(d) * 2 + c
        c_ag(d, f, i).wait_send()
        c_rz(d).wait_send()
        c_sib(0, d, fb, i).wait_send()
        for e in range(1, I):
            c_plane(e, d, fb, i).wait_send()
            c_sib(e, d, fb, ifrom(e)).wait_send()
        return carry

    def drain_g(d, carry):
        c_g(d).wait_send()
        for e in range(1, I):
            c_rp(e, d).wait_send()
        return carry

    c_own(f).wait_send()
    lax.fori_loop(1, Z, drain_z, 0)
    lax.fori_loop(0, Z, drain_g, 0)
    for e in range(1, I):
        c_fin(e, i).wait_send()

    def drain_tg(k, carry):
        c_tg(k).wait()
        return carry

    lax.fori_loop(0, 2 * Z, drain_tg, 0)

    def drain_out(k, carry):
        out_np(k).wait()
        out_nm(k).wait()
        return carry

    lax.fori_loop(0, I, drain_out, 0)
    out_val.wait()


def local(Z, I, tokens, upstream, params, momentum, projection):
    T, D = tokens.shape
    R, KV = params.shape
    PR = projection.shape[1]
    q = R // I
    V = pltpu.VMEM
    dma = pltpu.SemaphoreType.DMA
    any_spec = pl.BlockSpec(memory_space=pl.ANY)
    outs = pl.pallas_call(
        functools.partial(kernel, Z, I),
        out_shape=(
            jax.ShapeDtypeStruct((T, KV), BF16),
            jax.ShapeDtypeStruct((T, D), BF16),
            jax.ShapeDtypeStruct((I, q, KV), F32),
            jax.ShapeDtypeStruct((I, q, KV), F32),
        ),
        in_specs=[any_spec] * 5,
        out_specs=(any_spec,) * 4,
        scratch_shapes=[
            V((T, D), BF16), V((T, KV), BF16), V((I, q, KV), F32), V((I, q, KV), F32), V((KV, PR), F32), V((KV, PR), BF16),
            V((2 * Z, I, q, KV), BF16), V((T, PR), BF16),
            V((Z, R, PR), BF16), V((Z, R, PR), BF16), V((Z, I, q, PR), BF16),
            V((I, Z, q, PR), BF16), V((Z, q, PR), BF16), V((Z, q, PR), BF16), V((I, q, PR), BF16),
            V((T, KV), F32), V((T, KV), BF16), V((2 * Z, T, R), BF16), V((I, q, KV), F32),
            dma((5,)), dma, dma((2 * Z,)), dma((I,)), dma((I,)),
            dma, dma, dma((Z,)), dma((Z,)), dma((I, Z)), dma((I, Z)), dma((I, Z)), dma((I, Z)),
            dma((Z,)), dma((Z,)), dma((I, Z)), dma((I, Z)), dma((Z,)), dma((Z,)), dma((I,)), dma((I,)),
        ],
        compiler_params=pltpu.CompilerParams(collective_id=0, has_side_effects=True, vmem_limit_bytes=56 * 2**20),
    )(tokens, upstream, params.reshape(I, q, KV), momentum.reshape(I, q, KV), projection)
    values, grads, new_params, new_momentum = outs
    return (values, grads, new_params.reshape(R, KV), new_momentum.reshape(R, KV))


def solution(mesh):
    I, F = mesh.shape["island"], mesh.shape["fsdp"]
    rows, shard, whole = P(("island", "fsdp"), None), P("fsdp", None), P()
    return jax.shard_map(
        functools.partial(local, F // 2, I), mesh=mesh,
        in_specs=(rows, rows, shard, shard, whole), out_specs=(rows, rows, shard, shard), check_vma=False,
    )
```

```python
import functools
import math

import jax
import jax.numpy as jnp
from jax import lax
from jax.experimental import pallas as pl
from jax.experimental.pallas import tpu as pltpu
from jax.sharding import PartitionSpec as P

MESH = pl.DeviceIdType.MESH
F32 = jnp.float32
BF16 = jnp.bfloat16


def kernel(Z, I, tok_h, up_h, par_h, mom_h, proj_h, val_h, tg_h, np_h, nm_h,
           tok, up, par, mom, proj, projb, w, s, gsend, grecv, h, pb, zb, zr, fin, acc, val, tg, nm,
           in_sem, out_sem, tg_sem, np_sem, nm_sem,
           own_s, own_r, ag_s, ag_r, pl_s, pl_r, sib_s, sib_r, agd_s, agd_r, sibd_s, sibd_r, pld_s, pld_r, sibl_s, sibl_r, g_s, g_r, rp_s, rp_r, rz_s, rz_r, f_s, f_r):
    i = lax.axis_index("island")
    f = lax.axis_index("fsdp")
    z, c = f // 2, f % 2
    o = 1 - c
    sib = (i, z * 2 + o)
    R, KV = w.shape[1] * w.shape[2], w.shape[3]
    inv_width = 1.0 / math.sqrt(tok.shape[1])

    def zto(d):
        return lax.rem(z + d, Z)

    def zfrom(d):
        return lax.rem(z - d + Z, Z)

    def ito(e):
        return lax.rem(i + e, I)

    def ifrom(e):
        return lax.rem(i - e + I, I)

    ins = [pltpu.make_async_copy(a, b, in_sem.at[k]) for k, (a, b) in enumerate(
        ((par_h, par), (up_h, up), (proj_h, proj), (tok_h, tok), (mom_h, mom)))]
    for cp in ins:
        cp.start()

    barrier = pltpu.get_barrier_semaphore()
    for d in range(1, Z):
        pl.semaphore_signal(barrier, inc=1, device_id=(i, zto(d) * 2 + c), device_id_type=MESH)
    for e in range(1, I):
        pl.semaphore_signal(barrier, inc=1, device_id=(ito(e), f), device_id_type=MESH)
    pl.semaphore_signal(barrier, inc=1, device_id=sib, device_id_type=MESH)

    def remote(src, dst, ss, rs, to):
        return pltpu.make_async_remote_copy(src_ref=src, dst_ref=dst, send_sem=ss, recv_sem=rs, device_id=to, device_id_type=MESH)

    def c_own(fb):
        return remote(w.at[fb], w.at[fb], own_s, own_r, sib)

    def c_ag(d, fb, part):
        return remote(w.at[fb, part], w.at[fb, part], ag_s.at[d], ag_r.at[d], (i, zto(d) * 2 + c))

    def c_plane(e, d, fb, part):
        return remote(w.at[fb, part], w.at[fb, part], pl_s.at[e, d], pl_r.at[e, d], (ito(e), f))

    def c_sib(e, d, fb, part):
        return remote(w.at[fb, part], w.at[fb, part], sib_s.at[e, d], sib_r.at[e, d], sib)

    q = w.shape[2]
    cut = q // 32 * 16
    far = I - 1 - i
    upper, lower = pl.ds(0, cut), pl.ds(cut, q - cut)

    def c_agd(d, fb):
        return remote(w.at[fb, far, upper], w.at[fb, far, upper], agd_s.at[d], agd_r.at[d], (i, zto(d) * 2 + c))

    def c_sibd(d, fb, part):
        return remote(w.at[fb, part, upper], w.at[fb, part, upper], sibd_s.at[d], sibd_r.at[d], sib)

    def c_planed(d, fb, part):
        return remote(w.at[fb, part, lower], w.at[fb, part, lower], pld_s.at[d], pld_r.at[d], (far, f))

    def c_sibl(d, fb, part):
        return remote(w.at[fb, part, lower], w.at[fb, part, lower], sibl_s.at[d], sibl_r.at[d], sib)

    def c_g(d):
        return remote(gsend.at[d], grecv.at[d], g_s.at[d], g_r.at[d], sib)

    def c_rp(e, d):
        return remote(h.at[d, ito(e)], pb.at[e, d], rp_s.at[e, d], rp_r.at[e, d], (ito(e), f))

    def c_rz(d):
        return remote(zb.at[d], zr.at[d], rz_s.at[d], rz_r.at[d], (i, zto(d) * 2 + c))

    def c_fin(e, part):
        return remote(fin.at[part], fin.at[part], f_s.at[e], f_r.at[e], (ito(e), f))

    ins[0].wait()
    w[f] = par[...].astype(BF16)
    pl.semaphore_wait(barrier, Z + I - 1)
    for d in range(1, Z):
        c_ag(d, f, i).start()
    if cut:
        for d in range(1, Z):
            c_agd(d, f).start()
    c_own(f).start()

    ins[1].wait()
    ins[2].wait()
    projb[...] = proj[...].astype(BF16)
    s[...] = jnp.dot(up[...], projb[...], preferred_element_type=F32).astype(BF16)
    ins[3].wait()

    def cols(fb):
        return pl.ds(pl.multiple_of(fb * R, R), R)

    def gblock(fb):
        return lax.dot_general(tok[:, cols(fb)], s[...], (((0,), (0,)), ((), ())), preferred_element_type=F32)

    def send_g(d, carry):
        gsend[d] = gblock(zto(d) * 2 + o).astype(BF16)
        c_g(d).start()
        return carry

    lax.fori_loop(0, Z, send_g, 0)

    def send_rp(d, carry):
        mine = gblock(zto(d) * 2 + c)
        c_g(d).wait_recv()
        h[d] = (mine + grecv[d].astype(F32)).astype(BF16).reshape(h.shape[1:])
        for e in range(1, I):
            c_rp(e, d).start()
        return carry

    lax.fori_loop(0, Z, send_rp, 0)

    acc[...] = jnp.zeros_like(acc)

    def c_tg(fb):
        return pltpu.make_async_copy(tg.at[fb], tg_h.at[:, cols(fb)], tg_sem.at[fb])

    def block(fb):
        wb = w[fb].reshape(R, KV)
        acc[...] += jnp.dot(tok[:, cols(fb)], wb, preferred_element_type=F32)
        product = lax.dot_general(up[...], wb, (((1,), (1,)), ((), ())), preferred_element_type=F32)
        tg[fb] = (product * inv_width).astype(BF16)
        c_tg(fb).start()

    def forward(d, carry):
        fb = zfrom(d) * 2 + c
        c_ag(d, fb, i).wait_recv()
        for e in range(1, I):
            @pl.when(ito(e) != far)
            def _():
                c_plane(e, d, fb, i).start()

        c_planed(d, fb, i).start()
        c_sib(0, d, fb, i).start()
        return carry

    lax.fori_loop(1, Z, forward, 0)

    def send_rz(d, carry):
        total = h[d, i].astype(F32)
        for e in range(1, I):
            c_rp(e, d).wait_recv()
            total += pb[e, d].astype(F32)
        zb[d] = total.astype(BF16)

        @pl.when(d > 0)
        def _():
            c_rz(d).start()

        return carry

    lax.fori_loop(0, Z, send_rz, 0)

    block(f)
    c_own(z * 2 + o).wait_recv()
    block(z * 2 + o)

    total = zb[0].astype(F32)
    for d in range(1, Z):
        c_rz(d).wait_recv()
        total += zr[d].astype(F32)
    fin[i] = total.astype(BF16)
    for e in range(1, I):
        c_fin(e, i).start()

    factor = 1.0 / (math.sqrt(tok.shape[0] * 2 * Z) * projb.shape[1] * I)
    ins[4].wait()

    def out_np(part):
        return pltpu.make_async_copy(par.at[part], np_h.at[part], np_sem.at[part])

    def out_nm(part):
        return pltpu.make_async_copy(nm.at[part], nm_h.at[part], nm_sem.at[part])

    def finish(e, carry):
        part = ifrom(e)

        @pl.when(e > 0)
        def _():
            c_fin(e, part).wait_recv()

        outer = lax.dot_general(fin[part], projb[...], (((1,), (1,)), ((), ())), preferred_element_type=F32) * factor
        new_momentum = 0.9 * mom[part] + outer
        nm[part] = new_momentum
        par[part] = par[part] - 0.7 * (outer + 0.9 * new_momentum)
        out_np(part).start()
        out_nm(part).start()
        return carry

    def arrive(d):
        fb = zfrom(d) * 2 + c
        if cut:
            c_agd(d, fb).wait_recv()
            c_sibd(d, fb, far).start()
        for e in range(1, I):
            @pl.when(ifrom(e) != far)
            def _():
                c_plane(e, d, fb, ifrom(e)).wait_recv()
                c_sib(e, d, fb, ifrom(e)).start()

        c_planed(d, fb, far).wait_recv()
        c_sibl(d, fb, far).start()

    def use(d):
        block(zfrom(d) * 2 + c)
        fo = zfrom(d) * 2 + o
        for e in range(I):
            @pl.when(ifrom(e) != far)
            def _():
                c_sib(e, d, fo, ifrom(e)).wait_recv()

        if cut:
            c_sibd(d, fo, far).wait_recv()
        c_sibl(d, fo, far).wait_recv()
        block(fo)

    def take(d, carry):
        arrive(d)
        use(d)
        return carry

    lax.fori_loop(1, Z - 1, take, 0)
    arrive(Z - 1)
    lax.fori_loop(0, I, finish, 0)
    use(Z - 1)
    val[...] = (acc[...] * inv_width).astype(BF16)
    out_val = pltpu.make_async_copy(val, val_h, out_sem)
    out_val.start()

    def drain_z(d, carry):
        fb = zfrom(d) * 2 + c
        c_ag(d, f, i).wait_send()
        c_rz(d).wait_send()
        c_sib(0, d, fb, i).wait_send()
        for e in range(1, I):
            @pl.when(ito(e) != far)
            def _():
                c_plane(e, d, fb, i).wait_send()

            @pl.when(ifrom(e) != far)
            def _():
                c_sib(e, d, fb, ifrom(e)).wait_send()

        if cut:
            c_agd(d, f).wait_send()
            c_sibd(d, fb, far).wait_send()
        c_planed(d, fb, i).wait_send()
        c_sibl(d, fb, far).wait_send()
        return carry

    def drain_g(d, carry):
        c_g(d).wait_send()
        for e in range(1, I):
            c_rp(e, d).wait_send()
        return carry

    c_own(f).wait_send()
    lax.fori_loop(1, Z, drain_z, 0)
    lax.fori_loop(0, Z, drain_g, 0)
    for e in range(1, I):
        c_fin(e, i).wait_send()

    def drain_tg(k, carry):
        c_tg(k).wait()
        return carry

    lax.fori_loop(0, 2 * Z, drain_tg, 0)

    def drain_out(k, carry):
        out_np(k).wait()
        out_nm(k).wait()
        return carry

    lax.fori_loop(0, I, drain_out, 0)
    out_val.wait()


def local(Z, I, tokens, upstream, params, momentum, projection):
    T, D = tokens.shape
    R, KV = params.shape
    PR = projection.shape[1]
    q = R // I
    V = pltpu.VMEM
    dma = pltpu.SemaphoreType.DMA
    any_spec = pl.BlockSpec(memory_space=pl.ANY)
    outs = pl.pallas_call(
        functools.partial(kernel, Z, I),
        out_shape=(
            jax.ShapeDtypeStruct((T, KV), BF16),
            jax.ShapeDtypeStruct((T, D), BF16),
            jax.ShapeDtypeStruct((I, q, KV), F32),
            jax.ShapeDtypeStruct((I, q, KV), F32),
        ),
        in_specs=[pl.BlockSpec(memory_space=pltpu.HBM)] * 5,
        out_specs=(any_spec,) * 4,
        scratch_shapes=[
            V((T, D), BF16), V((T, KV), BF16), V((I, q, KV), F32), V((I, q, KV), F32), V((KV, PR), F32), V((KV, PR), BF16),
            V((2 * Z, I, q, KV), BF16), V((T, PR), BF16),
            V((Z, R, PR), BF16), V((Z, R, PR), BF16), V((Z, I, q, PR), BF16),
            V((I, Z, q, PR), BF16), V((Z, q, PR), BF16), V((Z, q, PR), BF16), V((I, q, PR), BF16),
            V((T, KV), F32), V((T, KV), BF16), V((2 * Z, T, R), BF16), V((I, q, KV), F32),
            dma((5,)), dma, dma((2 * Z,)), dma((I,)), dma((I,)),
            dma, dma, dma((Z,)), dma((Z,)), dma((I, Z)), dma((I, Z)), dma((I, Z)), dma((I, Z)),
            *[dma((Z,))] * 8,
            dma((Z,)), dma((Z,)), dma((I, Z)), dma((I, Z)), dma((Z,)), dma((Z,)), dma((I,)), dma((I,)),
        ],
        compiler_params=pltpu.CompilerParams(collective_id=0, has_side_effects=True, vmem_limit_bytes=46 * 2**20),
    )(tokens, upstream, params.reshape(I, q, KV), momentum.reshape(I, q, KV), projection)
    values, grads, new_params, new_momentum = outs
    return (values, grads, new_params.reshape(R, KV), new_momentum.reshape(R, KV))


def solution(mesh):
    I, F = mesh.shape["island"], mesh.shape["fsdp"]
    rows, shard, whole = P(("island", "fsdp"), None), P("fsdp", None), P()
    return jax.shard_map(
        functools.partial(local, F // 2, I), mesh=mesh,
        in_specs=(rows, rows, shard, shard, whole), out_specs=(rows, rows, shard, shard), check_vma=False,
    )
```

```python
import functools
import math

import jax
import jax.numpy as jnp
from jax import lax
from jax.experimental import pallas as pl
from jax.experimental.pallas import tpu as pltpu
from jax.sharding import PartitionSpec as P

MESH = pl.DeviceIdType.MESH
F32 = jnp.float32
BF16 = jnp.bfloat16


def kernel(Z, I, tok_h, up_h, par_h, mom_h, proj_h, val_h, tg_h, np_h, nm_h,
           tok, up, par, mom, proj, projb, w, s, gsend, grecv, h, pb, zb, zr, fin, acc, val, tg, nm,
           in_sem, out_sem, tg_sem, np_sem, nm_sem,
           own_s, own_r, ag_s, ag_r, pl_s, pl_r, sib_s, sib_r, agd_s, agd_r, sibd_s, sibd_r, pld_s, pld_r, sibl_s, sibl_r, g_s, g_r, rp_s, rp_r, rz_s, rz_r, f_s, f_r):
    i = lax.axis_index("island")
    f = lax.axis_index("fsdp")
    z, c = f // 2, f % 2
    o = 1 - c
    sib = (i, z * 2 + o)
    R, KV = w.shape[1] * w.shape[2], w.shape[3]
    inv_width = 1.0 / math.sqrt(tok.shape[1])

    def zto(d):
        return lax.rem(z + d, Z)

    def zfrom(d):
        return lax.rem(z - d + Z, Z)

    def ito(e):
        return lax.rem(i + e, I)

    def ifrom(e):
        return lax.rem(i - e + I, I)

    ins = [pltpu.make_async_copy(a, b, in_sem.at[k]) for k, (a, b) in enumerate(
        ((par_h, par), (up_h, up), (proj_h, proj), (tok_h, tok), (mom_h, mom)))]
    for cp in ins[:4]:
        cp.start()

    barrier = pltpu.get_barrier_semaphore()
    for d in range(1, Z):
        pl.semaphore_signal(barrier, inc=1, device_id=(i, zto(d) * 2 + c), device_id_type=MESH)
    for e in range(1, I):
        pl.semaphore_signal(barrier, inc=1, device_id=(ito(e), f), device_id_type=MESH)
    pl.semaphore_signal(barrier, inc=1, device_id=sib, device_id_type=MESH)

    def remote(src, dst, ss, rs, to):
        return pltpu.make_async_remote_copy(src_ref=src, dst_ref=dst, send_sem=ss, recv_sem=rs, device_id=to, device_id_type=MESH)

    def c_own(fb):
        return remote(w.at[fb], w.at[fb], own_s, own_r, sib)

    def c_ag(d, fb, part):
        return remote(w.at[fb, part], w.at[fb, part], ag_s.at[d], ag_r.at[d], (i, zto(d) * 2 + c))

    def c_plane(e, d, fb, part):
        return remote(w.at[fb, part], w.at[fb, part], pl_s.at[e, d], pl_r.at[e, d], (ito(e), f))

    def c_sib(e, d, fb, part):
        return remote(w.at[fb, part], w.at[fb, part], sib_s.at[e, d], sib_r.at[e, d], sib)

    q = w.shape[2]
    cut = q // 32 * 16
    far = I - 1 - i
    upper, lower = pl.ds(0, cut), pl.ds(cut, q - cut)

    def c_agd(d, fb):
        return remote(w.at[fb, far, upper], w.at[fb, far, upper], agd_s.at[d], agd_r.at[d], (i, zto(d) * 2 + c))

    def c_sibd(d, fb, part):
        return remote(w.at[fb, part, upper], w.at[fb, part, upper], sibd_s.at[d], sibd_r.at[d], sib)

    def c_planed(d, fb, part):
        return remote(w.at[fb, part, lower], w.at[fb, part, lower], pld_s.at[d], pld_r.at[d], (far, f))

    def c_sibl(d, fb, part):
        return remote(w.at[fb, part, lower], w.at[fb, part, lower], sibl_s.at[d], sibl_r.at[d], sib)

    def c_g(d):
        return remote(gsend.at[d], grecv.at[d], g_s.at[d], g_r.at[d], sib)

    def c_rp(e, d):
        return remote(h.at[d, ito(e)], pb.at[e, d], rp_s.at[e, d], rp_r.at[e, d], (ito(e), f))

    two_stage = I == 4
    beside, across = i + 1 - 2 * lax.rem(i, 2), lax.rem(i + 2, I)

    def pair(d):
        turn = lax.rem(d, 2) * (across - beside)
        return beside + turn, across - turn

    def c_r1(d, k):
        first, _ = pair(d)
        return remote(h.at[d, far if k else first], pb.at[1 + k, d], rp_s.at[1 + k, d], rp_r.at[1 + k, d], (first, f))

    def c_r2(d):
        _, second = pair(d)
        return remote(h.at[d, second], pb.at[3, d], rp_s.at[3, d], rp_r.at[3, d], (second, f))

    def stage2(d, carry):
        _, second = pair(d)
        c_r1(d, 1).wait_recv()
        h[d, second] = (h[d, second].astype(F32) + pb[2, d].astype(F32)).astype(BF16)
        c_r2(d).start()
        return carry

    def c_rz(d):
        return remote(zb.at[d], zr.at[d], rz_s.at[d], rz_r.at[d], (i, zto(d) * 2 + c))

    def c_fin(e, part):
        return remote(fin.at[part], fin.at[part], f_s.at[e], f_r.at[e], (ito(e), f))

    ins[0].wait()
    w[f] = par[...].astype(BF16)
    pl.semaphore_wait(barrier, Z + I - 1)
    for d in range(1, Z):
        c_ag(d, f, i).start()
    c_own(f).start()

    ins[1].wait()
    ins[2].wait()
    projb[...] = proj[...].astype(BF16)
    s[...] = jnp.dot(up[...], projb[...], preferred_element_type=F32).astype(BF16)
    ins[3].wait()
    ins[4].start()

    def cols(fb):
        return pl.ds(pl.multiple_of(fb * R, R), R)

    def gblock(fb):
        return lax.dot_general(tok[:, cols(fb)], s[...], (((0,), (0,)), ((), ())), preferred_element_type=F32)

    def send_g(d):
        gsend[d] = gblock(zto(d) * 2 + o).astype(BF16)
        c_g(d).start()

    def send_rp(d):
        mine = gblock(zto(d) * 2 + c)
        c_g(d).wait_recv()
        h[d] = (mine + grecv[d].astype(F32)).astype(BF16).reshape(h.shape[1:])
        if two_stage:
            c_r1(d, 1).start()
            c_r1(d, 0).start()
        else:
            for e in range(1, I):
                c_rp(e, d).start()

    send_g(0)

    def sketch(d, carry):
        send_g(d)
        send_rp(d - 1)
        return carry

    lax.fori_loop(1, Z, sketch, 0)
    send_rp(Z - 1)
    if cut:
        for d in range(1, Z):
            c_agd(d, f).start()

    acc[...] = jnp.zeros_like(acc)

    def c_tg(fb):
        return pltpu.make_async_copy(tg.at[fb], tg_h.at[:, cols(fb)], tg_sem.at[fb])

    def block(fb):
        wb = w[fb].reshape(R, KV)
        acc[...] += jnp.dot(tok[:, cols(fb)], wb, preferred_element_type=F32)
        product = lax.dot_general(up[...], wb, (((1,), (1,)), ((), ())), preferred_element_type=F32)
        tg[fb] = (product * inv_width).astype(BF16)
        c_tg(fb).start()

    def forward(d, carry):
        fb = zfrom(d) * 2 + c
        c_ag(d, fb, i).wait_recv()
        for e in range(1, I):
            @pl.when(ito(e) != far)
            def _():
                c_plane(e, d, fb, i).start()

        c_planed(d, fb, i).start()
        c_sib(0, d, fb, i).start()
        return carry

    if two_stage:
        lax.fori_loop(0, Z // 2, stage2, 0)
        lax.fori_loop(1, 2, forward, 0)
        lax.fori_loop(Z // 2, Z, stage2, 0)
        lax.fori_loop(2, Z, forward, 0)
    else:
        lax.fori_loop(1, Z, forward, 0)

    def send_rz(d, carry):
        total = h[d, i].astype(F32)
        if two_stage:
            c_r1(d, 0).wait_recv()
            c_r2(d).wait_recv()
            total += pb[1, d].astype(F32) + pb[3, d].astype(F32)
        else:
            for e in range(1, I):
                c_rp(e, d).wait_recv()
                total += pb[e, d].astype(F32)
        zb[d] = total.astype(BF16)

        @pl.when(d > 0)
        def _():
            c_rz(d).start()

        return carry

    lax.fori_loop(0, Z, send_rz, 0)

    block(f)
    c_own(z * 2 + o).wait_recv()
    block(z * 2 + o)

    total = zb[0].astype(F32)
    for d in range(1, Z):
        c_rz(d).wait_recv()
        total += zr[d].astype(F32)
    fin[i] = total.astype(BF16)
    for e in range(1, I):
        c_fin(e, i).start()

    factor = 1.0 / (math.sqrt(tok.shape[0] * 2 * Z) * projb.shape[1] * I)
    ins[4].wait()

    def out_np(part):
        return pltpu.make_async_copy(par.at[part], np_h.at[part], np_sem.at[part])

    def out_nm(part):
        return pltpu.make_async_copy(nm.at[part], nm_h.at[part], nm_sem.at[part])

    def finish(e, carry):
        part = ifrom(e)

        @pl.when(e > 0)
        def _():
            c_fin(e, part).wait_recv()

        outer = lax.dot_general(fin[part], projb[...], (((1,), (1,)), ((), ())), preferred_element_type=F32) * factor
        new_momentum = 0.9 * mom[part] + outer
        nm[part] = new_momentum
        par[part] = par[part] - 0.7 * (outer + 0.9 * new_momentum)
        out_np(part).start()
        out_nm(part).start()
        return carry

    def arrive(d):
        fb = zfrom(d) * 2 + c
        if cut:
            c_agd(d, fb).wait_recv()
            c_sibd(d, fb, far).start()
        for e in range(1, I):
            @pl.when(ifrom(e) != far)
            def _():
                c_plane(e, d, fb, ifrom(e)).wait_recv()
                c_sib(e, d, fb, ifrom(e)).start()

        c_planed(d, fb, far).wait_recv()
        c_sibl(d, fb, far).start()

    def use(d):
        block(zfrom(d) * 2 + c)
        fo = zfrom(d) * 2 + o
        for e in range(I):
            @pl.when(ifrom(e) != far)
            def _():
                c_sib(e, d, fo, ifrom(e)).wait_recv()

        if cut:
            c_sibd(d, fo, far).wait_recv()
        c_sibl(d, fo, far).wait_recv()
        block(fo)

    def take(d, carry):
        arrive(d)
        use(d)
        return carry

    lax.fori_loop(1, Z - 1, take, 0)
    arrive(Z - 1)
    lax.fori_loop(0, I, finish, 0)
    use(Z - 1)
    val[...] = (acc[...] * inv_width).astype(BF16)
    out_val = pltpu.make_async_copy(val, val_h, out_sem)
    out_val.start()

    def drain_z(d, carry):
        fb = zfrom(d) * 2 + c
        c_ag(d, f, i).wait_send()
        c_rz(d).wait_send()
        c_sib(0, d, fb, i).wait_send()
        for e in range(1, I):
            @pl.when(ito(e) != far)
            def _():
                c_plane(e, d, fb, i).wait_send()

            @pl.when(ifrom(e) != far)
            def _():
                c_sib(e, d, fb, ifrom(e)).wait_send()

        if cut:
            c_agd(d, f).wait_send()
            c_sibd(d, fb, far).wait_send()
        c_planed(d, fb, i).wait_send()
        c_sibl(d, fb, far).wait_send()
        return carry

    def drain_g(d, carry):
        c_g(d).wait_send()
        if two_stage:
            c_r1(d, 0).wait_send()
            c_r1(d, 1).wait_send()
            c_r2(d).wait_send()
        else:
            for e in range(1, I):
                c_rp(e, d).wait_send()
        return carry

    c_own(f).wait_send()
    lax.fori_loop(1, Z, drain_z, 0)
    lax.fori_loop(0, Z, drain_g, 0)
    for e in range(1, I):
        c_fin(e, i).wait_send()

    def drain_tg(k, carry):
        c_tg(k).wait()
        return carry

    lax.fori_loop(0, 2 * Z, drain_tg, 0)

    def drain_out(k, carry):
        out_np(k).wait()
        out_nm(k).wait()
        return carry

    lax.fori_loop(0, I, drain_out, 0)
    out_val.wait()


def local(Z, I, tokens, upstream, params, momentum, projection):
    T, D = tokens.shape
    R, KV = params.shape
    PR = projection.shape[1]
    q = R // I
    V = pltpu.VMEM
    dma = pltpu.SemaphoreType.DMA
    any_spec = pl.BlockSpec(memory_space=pl.ANY)
    outs = pl.pallas_call(
        functools.partial(kernel, Z, I),
        out_shape=(
            jax.ShapeDtypeStruct((T, KV), BF16),
            jax.ShapeDtypeStruct((T, D), BF16),
            jax.ShapeDtypeStruct((I, q, KV), F32),
            jax.ShapeDtypeStruct((I, q, KV), F32),
        ),
        in_specs=[pl.BlockSpec(memory_space=pltpu.HBM)] * 5,
        out_specs=(any_spec,) * 4,
        scratch_shapes=[
            V((T, D), BF16), V((T, KV), BF16), V((I, q, KV), F32), V((I, q, KV), F32), V((KV, PR), F32), V((KV, PR), BF16),
            V((2 * Z, I, q, KV), BF16), V((T, PR), BF16),
            V((Z, R, PR), BF16), V((Z, R, PR), BF16), V((Z, I, q, PR), BF16),
            V((I, Z, q, PR), BF16), V((Z, q, PR), BF16), V((Z, q, PR), BF16), V((I, q, PR), BF16),
            V((T, KV), F32), V((T, KV), BF16), V((2 * Z, T, R), BF16), V((I, q, KV), F32),
            dma((5,)), dma, dma((2 * Z,)), dma((I,)), dma((I,)),
            dma, dma, dma((Z,)), dma((Z,)), dma((I, Z)), dma((I, Z)), dma((I, Z)), dma((I, Z)),
            *[dma((Z,))] * 8,
            dma((Z,)), dma((Z,)), dma((I, Z)), dma((I, Z)), dma((Z,)), dma((Z,)), dma((I,)), dma((I,)),
        ],
        compiler_params=pltpu.CompilerParams(collective_id=0, has_side_effects=True, vmem_limit_bytes=46 * 2**20),
    )(tokens, upstream, params.reshape(I, q, KV), momentum.reshape(I, q, KV), projection)
    values, grads, new_params, new_momentum = outs
    return (values, grads, new_params.reshape(R, KV), new_momentum.reshape(R, KV))


def solution(mesh):
    I, F = mesh.shape["island"], mesh.shape["fsdp"]
    rows, shard, whole = P(("island", "fsdp"), None), P("fsdp", None), P()
    return jax.shard_map(
        functools.partial(local, F // 2, I), mesh=mesh,
        in_specs=(rows, rows, shard, shard, whole), out_specs=(rows, rows, shard, shard), check_vma=False,
    )
```

```python
import functools
import math

import jax
import jax.numpy as jnp
from jax import lax
from jax.experimental import pallas as pl
from jax.experimental.pallas import tpu as pltpu
from jax.sharding import PartitionSpec as P

MESH = pl.DeviceIdType.MESH
F32 = jnp.float32
BF16 = jnp.bfloat16


def kernel(Z, I, tok_h, up_h, par_h, mom_h, proj_h, val_h, tg_h, np_h, nm_h,
           tok, up, par, mom, proj, projb, w, s, gsend, grecv, h, pb, zb, zr, fin, acc, val, tg, nm,
           in_sem, out_sem, tg_sem, np_sem, nm_sem,
           own_s, own_r, ag_s, ag_r, pl_s, pl_r, sib_s, sib_r, agd_s, agd_r, sibd_s, sibd_r, pld_s, pld_r, sibl_s, sibl_r, g_s, g_r, rp_s, rp_r, rz_s, rz_r, f_s, f_r):
    i = lax.axis_index("island")
    f = lax.axis_index("fsdp")
    z, c = f // 2, f % 2
    o = 1 - c
    sib = (i, z * 2 + o)
    R, KV = w.shape[1] * w.shape[2], w.shape[3]
    inv_width = 1.0 / math.sqrt(tok.shape[1])

    def zto(d):
        return lax.rem(z + d, Z)

    def zfrom(d):
        return lax.rem(z - d + Z, Z)

    def ito(e):
        return lax.rem(i + e, I)

    def ifrom(e):
        return lax.rem(i - e + I, I)

    ins = [pltpu.make_async_copy(a, b, in_sem.at[k]) for k, (a, b) in enumerate(
        ((par_h, par), (up_h, up), (proj_h, proj), (tok_h, tok), (mom_h, mom)))]
    for cp in ins[:4]:
        cp.start()

    barrier = pltpu.get_barrier_semaphore()
    for d in range(1, Z):
        pl.semaphore_signal(barrier, inc=1, device_id=(i, zto(d) * 2 + c), device_id_type=MESH)
    for e in range(1, I):
        pl.semaphore_signal(barrier, inc=1, device_id=(ito(e), f), device_id_type=MESH)
    pl.semaphore_signal(barrier, inc=1, device_id=sib, device_id_type=MESH)

    def remote(src, dst, ss, rs, to):
        return pltpu.make_async_remote_copy(src_ref=src, dst_ref=dst, send_sem=ss, recv_sem=rs, device_id=to, device_id_type=MESH)

    def c_own(fb):
        return remote(w.at[fb], w.at[fb], own_s, own_r, sib)

    def c_ag(down, d, fb):
        to = lax.rem(z + (Z - 1 if down else 1), Z)
        return remote(w.at[fb, i], w.at[fb, i], ag_s.at[down * Z + d], ag_r.at[d], (i, to * 2 + c))

    def ag_own(act):
        @pl.when(z < Z - 1)
        def _():
            act(c_ag(0, 1, f))

        @pl.when(z > 0)
        def _():
            act(c_ag(1, Z - 1, f))

    def ag_relay_up(d, act):
        @pl.when(z < Z - 1)
        def _():
            act(c_ag(0, d + 1, zfrom(d) * 2 + c))

    def ag_relay_down(d, act):
        @pl.when(z > 0)
        def _():
            act(c_ag(1, d - 1, zfrom(d) * 2 + c))

    def c_plane(e, d, fb, part):
        return remote(w.at[fb, part], w.at[fb, part], pl_s.at[e, d], pl_r.at[e, d], (ito(e), f))

    def c_sib(e, d, fb, part):
        return remote(w.at[fb, part], w.at[fb, part], sib_s.at[e, d], sib_r.at[e, d], sib)

    q = w.shape[2]
    cut = q // 32 * 16
    far = I - 1 - i
    upper, lower = pl.ds(0, cut), pl.ds(cut, q - cut)

    def c_agd(d, fb):
        return remote(w.at[fb, far, upper], w.at[fb, far, upper], agd_s.at[d], agd_r.at[d], (i, zto(d) * 2 + c))

    def c_sibd(d, fb, part):
        return remote(w.at[fb, part, upper], w.at[fb, part, upper], sibd_s.at[d], sibd_r.at[d], sib)

    def c_planed(d, fb, part):
        return remote(w.at[fb, part, lower], w.at[fb, part, lower], pld_s.at[d], pld_r.at[d], (far, f))

    def c_sibl(d, fb, part):
        return remote(w.at[fb, part, lower], w.at[fb, part, lower], sibl_s.at[d], sibl_r.at[d], sib)

    def c_g(d):
        return remote(gsend.at[d], grecv.at[d], g_s.at[d], g_r.at[d], sib)

    def c_rp(e, d):
        return remote(h.at[d, ito(e)], pb.at[e, d], rp_s.at[e, d], rp_r.at[e, d], (ito(e), f))

    two_stage = I == 4
    beside, across = i + 1 - 2 * lax.rem(i, 2), lax.rem(i + 2, I)

    def pair(d):
        turn = lax.rem(d, 2) * (across - beside)
        return beside + turn, across - turn

    def c_r1(d, k):
        first, _ = pair(d)
        return remote(h.at[d, far if k else first], pb.at[1 + k, d], rp_s.at[1 + k, d], rp_r.at[1 + k, d], (first, f))

    def c_r2(d):
        _, second = pair(d)
        return remote(h.at[d, second], pb.at[3, d], rp_s.at[3, d], rp_r.at[3, d], (second, f))

    def stage2(d, carry):
        _, second = pair(d)
        c_r1(d, 1).wait_recv()
        h[d, second] = (h[d, second].astype(F32) + pb[2, d].astype(F32)).astype(BF16)
        c_r2(d).start()
        return carry

    def c_rz(d):
        return remote(zb.at[d], zr.at[d], rz_s.at[d], rz_r.at[d], (i, zto(d) * 2 + c))

    def c_fin(e, part):
        return remote(fin.at[part], fin.at[part], f_s.at[e], f_r.at[e], (ito(e), f))

    ins[0].wait()
    w[f] = par[...].astype(BF16)
    pl.semaphore_wait(barrier, Z + I - 1)
    ag_own(lambda copy: copy.start())
    c_own(f).start()

    ins[1].wait()
    ins[2].wait()
    projb[...] = proj[...].astype(BF16)
    s[...] = jnp.dot(up[...], projb[...], preferred_element_type=F32).astype(BF16)
    ins[3].wait()
    ins[4].start()

    def cols(fb):
        return pl.ds(pl.multiple_of(fb * R, R), R)

    def gblock(fb):
        return lax.dot_general(tok[:, cols(fb)], s[...], (((0,), (0,)), ((), ())), preferred_element_type=F32)

    def send_g(d):
        gsend[d] = gblock(zto(d) * 2 + o).astype(BF16)
        c_g(d).start()

    def send_rp(d):
        mine = gblock(zto(d) * 2 + c)
        c_g(d).wait_recv()
        h[d] = (mine + grecv[d].astype(F32)).astype(BF16).reshape(h.shape[1:])
        if two_stage:
            c_r1(d, 1).start()
            c_r1(d, 0).start()
        else:
            for e in range(1, I):
                c_rp(e, d).start()

    send_g(0)

    def sketch(d, carry):
        send_g(d)
        send_rp(d - 1)
        return carry

    lax.fori_loop(1, Z, sketch, 0)
    send_rp(Z - 1)
    acc[...] = jnp.zeros_like(acc)

    def c_tg(fb):
        return pltpu.make_async_copy(tg.at[fb], tg_h.at[:, cols(fb)], tg_sem.at[fb])

    def block(fb):
        wb = w[fb].reshape(R, KV)
        acc[...] += jnp.dot(tok[:, cols(fb)], wb, preferred_element_type=F32)
        product = lax.dot_general(up[...], wb, (((1,), (1,)), ((), ())), preferred_element_type=F32)
        tg[fb] = (product * inv_width).astype(BF16)
        c_tg(fb).start()

    def forward(d, up):
        fb = zfrom(d) * 2 + c
        c_ag(0 if up else 1, d, fb).wait_recv()
        (ag_relay_up if up else ag_relay_down)(d, lambda copy: copy.start())
        for e in range(1, I):
            @pl.when(ito(e) != far)
            def _():
                c_plane(e, d, fb, i).start()

        c_planed(d, fb, i).start()
        c_sib(0, d, fb, i).start()

    def hop(k, carry):
        @pl.when(z >= k)
        def _():
            forward(k, True)

        @pl.when(z + k < Z)
        def _():
            forward(Z - k, False)

        return carry

    lax.fori_loop(1, 2, hop, 0)
    if two_stage:
        lax.fori_loop(0, Z // 2, stage2, 0)
    lax.fori_loop(2, Z - 1, hop, 0)
    if cut:
        c_agd(1, f).start()
    if two_stage:
        lax.fori_loop(Z // 2, Z, stage2, 0)
    lax.fori_loop(max(2, Z - 1), Z, hop, 0)

    def send_rz(d, carry):
        total = h[d, i].astype(F32)
        if two_stage:
            c_r1(d, 0).wait_recv()
            c_r2(d).wait_recv()
            total += pb[1, d].astype(F32) + pb[3, d].astype(F32)
        else:
            for e in range(1, I):
                c_rp(e, d).wait_recv()
                total += pb[e, d].astype(F32)
        zb[d] = total.astype(BF16)

        @pl.when(d > 0)
        def _():
            c_rz(d).start()

        return carry

    lax.fori_loop(0, Z, send_rz, 0)
    if cut:
        for d in range(2, Z):
            c_agd(d, f).start()

    block(f)
    c_own(z * 2 + o).wait_recv()
    block(z * 2 + o)

    total = zb[0].astype(F32)
    for d in range(1, Z):
        c_rz(d).wait_recv()
        total += zr[d].astype(F32)
    fin[i] = total.astype(BF16)
    for e in range(1, I):
        c_fin(e, i).start()

    factor = 1.0 / (math.sqrt(tok.shape[0] * 2 * Z) * projb.shape[1] * I)
    ins[4].wait()

    def out_np(part):
        return pltpu.make_async_copy(par.at[part], np_h.at[part], np_sem.at[part])

    def out_nm(part):
        return pltpu.make_async_copy(nm.at[part], nm_h.at[part], nm_sem.at[part])

    def finish(e, carry):
        part = ifrom(e)

        @pl.when(e > 0)
        def _():
            c_fin(e, part).wait_recv()

        outer = lax.dot_general(fin[part], projb[...], (((1,), (1,)), ((), ())), preferred_element_type=F32) * factor
        new_momentum = 0.9 * mom[part] + outer
        nm[part] = new_momentum
        par[part] = par[part] - 0.7 * (outer + 0.9 * new_momentum)
        out_np(part).start()
        out_nm(part).start()
        return carry

    def arrive(d):
        fb = zfrom(d) * 2 + c
        if cut:
            c_agd(d, fb).wait_recv()
            c_sibd(d, fb, far).start()
        for e in range(1, I):
            @pl.when(ifrom(e) != far)
            def _():
                c_plane(e, d, fb, ifrom(e)).wait_recv()
                c_sib(e, d, fb, ifrom(e)).start()

        c_planed(d, fb, far).wait_recv()
        c_sibl(d, fb, far).start()

    def use(d):
        block(zfrom(d) * 2 + c)
        fo = zfrom(d) * 2 + o
        for e in range(I):
            @pl.when(ifrom(e) != far)
            def _():
                c_sib(e, d, fo, ifrom(e)).wait_recv()

        if cut:
            c_sibd(d, fo, far).wait_recv()
        c_sibl(d, fo, far).wait_recv()
        block(fo)

    def take(d, carry):
        arrive(d)
        use(d)
        return carry

    lax.fori_loop(1, Z - 1, take, 0)
    arrive(Z - 1)
    lax.fori_loop(0, I, finish, 0)
    use(Z - 1)
    val[...] = (acc[...] * inv_width).astype(BF16)
    out_val = pltpu.make_async_copy(val, val_h, out_sem)
    out_val.start()

    def drain_z(d, carry):
        fb = zfrom(d) * 2 + c
        @pl.when(z >= d)
        def _():
            ag_relay_up(d, lambda copy: copy.wait_send())

        @pl.when(z < d)
        def _():
            ag_relay_down(d, lambda copy: copy.wait_send())

        c_rz(d).wait_send()
        c_sib(0, d, fb, i).wait_send()
        for e in range(1, I):
            @pl.when(ito(e) != far)
            def _():
                c_plane(e, d, fb, i).wait_send()

            @pl.when(ifrom(e) != far)
            def _():
                c_sib(e, d, fb, ifrom(e)).wait_send()

        if cut:
            c_agd(d, f).wait_send()
            c_sibd(d, fb, far).wait_send()
        c_planed(d, fb, i).wait_send()
        c_sibl(d, fb, far).wait_send()
        return carry

    def drain_g(d, carry):
        c_g(d).wait_send()
        if two_stage:
            c_r1(d, 0).wait_send()
            c_r1(d, 1).wait_send()
            c_r2(d).wait_send()
        else:
            for e in range(1, I):
                c_rp(e, d).wait_send()
        return carry

    c_own(f).wait_send()
    ag_own(lambda copy: copy.wait_send())
    lax.fori_loop(1, Z, drain_z, 0)
    lax.fori_loop(0, Z, drain_g, 0)
    for e in range(1, I):
        c_fin(e, i).wait_send()

    def drain_tg(k, carry):
        c_tg(k).wait()
        return carry

    lax.fori_loop(0, 2 * Z, drain_tg, 0)

    def drain_out(k, carry):
        out_np(k).wait()
        out_nm(k).wait()
        return carry

    lax.fori_loop(0, I, drain_out, 0)
    out_val.wait()


def local(Z, I, tokens, upstream, params, momentum, projection):
    T, D = tokens.shape
    R, KV = params.shape
    PR = projection.shape[1]
    q = R // I
    V = pltpu.VMEM
    dma = pltpu.SemaphoreType.DMA
    any_spec = pl.BlockSpec(memory_space=pl.ANY)
    outs = pl.pallas_call(
        functools.partial(kernel, Z, I),
        out_shape=(
            jax.ShapeDtypeStruct((T, KV), BF16),
            jax.ShapeDtypeStruct((T, D), BF16),
            jax.ShapeDtypeStruct((I, q, KV), F32),
            jax.ShapeDtypeStruct((I, q, KV), F32),
        ),
        in_specs=[pl.BlockSpec(memory_space=pltpu.HBM)] * 5,
        out_specs=(any_spec,) * 4,
        scratch_shapes=[
            V((T, D), BF16), V((T, KV), BF16), V((I, q, KV), F32), V((I, q, KV), F32), V((KV, PR), F32), V((KV, PR), BF16),
            V((2 * Z, I, q, KV), BF16), V((T, PR), BF16),
            V((Z, R, PR), BF16), V((Z, R, PR), BF16), V((Z, I, q, PR), BF16),
            V((I, Z, q, PR), BF16), V((Z, q, PR), BF16), V((Z, q, PR), BF16), V((I, q, PR), BF16),
            V((T, KV), F32), V((T, KV), BF16), V((2 * Z, T, R), BF16), V((I, q, KV), F32),
            dma((5,)), dma, dma((2 * Z,)), dma((I,)), dma((I,)),
            dma, dma, dma((2 * Z,)), dma((Z,)), dma((I, Z)), dma((I, Z)), dma((I, Z)), dma((I, Z)),
            *[dma((Z,))] * 8,
            dma((Z,)), dma((Z,)), dma((I, Z)), dma((I, Z)), dma((Z,)), dma((Z,)), dma((I,)), dma((I,)),
        ],
        compiler_params=pltpu.CompilerParams(collective_id=0, has_side_effects=True, vmem_limit_bytes=46 * 2**20),
    )(tokens, upstream, params.reshape(I, q, KV), momentum.reshape(I, q, KV), projection)
    values, grads, new_params, new_momentum = outs
    return (values, grads, new_params.reshape(R, KV), new_momentum.reshape(R, KV))


def solution(mesh):
    I, F = mesh.shape["island"], mesh.shape["fsdp"]
    rows, shard, whole = P(("island", "fsdp"), None), P("fsdp", None), P()
    return jax.shard_map(
        functools.partial(local, F // 2, I), mesh=mesh,
        in_specs=(rows, rows, shard, shard, whole), out_specs=(rows, rows, shard, shard), check_vma=False,
    )
```

```python
import functools
import math

import jax
import jax.numpy as jnp
from jax import lax
from jax.experimental import pallas as pl
from jax.experimental.pallas import tpu as pltpu
from jax.sharding import PartitionSpec as P

MESH = pl.DeviceIdType.MESH
F32 = jnp.float32
BF16 = jnp.bfloat16


def kernel(Z, I, tok_h, up_h, par_h, mom_h, proj_h, val_h, tg_h, np_h, nm_h,
           tok, up, par, mom, proj, projb, w, s, gsend, grecv, h, pb, zb, zr, fin, acc, val, tg, nm,
           in_sem, out_sem, tg_sem, np_sem, nm_sem,
           own_s, own_r, ag_s, ag_r, pl_s, pl_r, sib_s, sib_r, agd_s, agd_r, sibd_s, sibd_r, pld_s, pld_r, sibl_s, sibl_r, g_s, g_r, rp_s, rp_r, rz_s, rz_r, f_s, f_r):
    i = lax.axis_index("island")
    f = lax.axis_index("fsdp")
    z, c = f // 2, f % 2
    o = 1 - c
    sib = (i, z * 2 + o)
    R, KV = w.shape[1] * w.shape[2], w.shape[3]
    inv_width = 1.0 / math.sqrt(tok.shape[1])

    def zto(d):
        return lax.rem(z + d, Z)

    def zfrom(d):
        return lax.rem(z - d + Z, Z)

    def ito(e):
        return lax.rem(i + e, I)

    def ifrom(e):
        return lax.rem(i - e + I, I)

    ins = [pltpu.make_async_copy(a, b, in_sem.at[k]) for k, (a, b) in enumerate(
        ((par_h, par), (up_h, up), (proj_h, proj), (tok_h, tok), (mom_h, mom)))]
    for cp in ins[:4]:
        cp.start()

    barrier = pltpu.get_barrier_semaphore()
    for d in range(1, Z):
        pl.semaphore_signal(barrier, inc=1, device_id=(i, zto(d) * 2 + c), device_id_type=MESH)
    for e in range(1, I):
        pl.semaphore_signal(barrier, inc=1, device_id=(ito(e), f), device_id_type=MESH)
    pl.semaphore_signal(barrier, inc=1, device_id=sib, device_id_type=MESH)

    def remote(src, dst, ss, rs, to):
        return pltpu.make_async_remote_copy(src_ref=src, dst_ref=dst, send_sem=ss, recv_sem=rs, device_id=to, device_id_type=MESH)

    def c_own(fb):
        return remote(w.at[fb], w.at[fb], own_s, own_r, sib)

    def c_ag(d, fb, part):
        return remote(w.at[fb, part], w.at[fb, part], ag_s.at[d], ag_r.at[d], (i, zto(d) * 2 + c))

    def c_plane(e, d, fb, part):
        return remote(w.at[fb, part], w.at[fb, part], pl_s.at[e, d], pl_r.at[e, d], (ito(e), f))

    def c_sib(e, d, fb, part):
        return remote(w.at[fb, part], w.at[fb, part], sib_s.at[e, d], sib_r.at[e, d], sib)

    q = w.shape[2]
    cut = q // 32 * 16
    far = I - 1 - i
    upper, lower = pl.ds(0, cut), pl.ds(cut, q - cut)

    def c_agd(d, fb):
        return remote(w.at[fb, far, upper], w.at[fb, far, upper], agd_s.at[d], agd_r.at[d], (i, zto(d) * 2 + c))

    def c_sibd(d, fb, part):
        return remote(w.at[fb, part, upper], w.at[fb, part, upper], sibd_s.at[d], sibd_r.at[d], sib)

    def c_planed(d, fb, part):
        return remote(w.at[fb, part, lower], w.at[fb, part, lower], pld_s.at[d], pld_r.at[d], (far, f))

    def c_sibl(d, fb, part):
        return remote(w.at[fb, part, lower], w.at[fb, part, lower], sibl_s.at[d], sibl_r.at[d], sib)

    def c_g(d):
        return remote(gsend.at[d], grecv.at[d], g_s.at[d], g_r.at[d], sib)

    def c_rp(e, d):
        return remote(h.at[d, ito(e)], pb.at[e, d], rp_s.at[e, d], rp_r.at[e, d], (ito(e), f))

    two_stage = I == 4
    beside, across = i + 1 - 2 * lax.rem(i, 2), lax.rem(i + 2, I)

    def pair(d):
        turn = lax.rem(d, 2) * (across - beside)
        return beside + turn, across - turn

    def c_r1(d, k):
        first, _ = pair(d)
        return remote(h.at[d, far if k else first], pb.at[1 + k, d], rp_s.at[1 + k, d], rp_r.at[1 + k, d], (first, f))

    def c_r2(d):
        _, second = pair(d)
        return remote(h.at[d, second], pb.at[3, d], rp_s.at[3, d], rp_r.at[3, d], (second, f))

    def stage2(d, carry):
        _, second = pair(d)
        c_r1(d, 1).wait_recv()
        h[d, second] = (h[d, second].astype(F32) + pb[2, d].astype(F32)).astype(BF16)
        c_r2(d).start()
        return carry

    def c_rz(d):
        return remote(zb.at[d], zr.at[d], rz_s.at[d], rz_r.at[d], (i, zto(d) * 2 + c))

    def c_fin(e, part):
        return remote(fin.at[part], fin.at[part], f_s.at[e], f_r.at[e], (ito(e), f))

    ins[0].wait()
    w[f] = par[...].astype(BF16)
    pl.semaphore_wait(barrier, Z + I - 1)
    for d in range(1, Z):
        c_ag(d, f, i).start()
    c_own(f).start()

    ins[1].wait()
    ins[2].wait()
    projb[...] = proj[...].astype(BF16)
    s[...] = jnp.dot(up[...], projb[...], preferred_element_type=F32).astype(BF16)
    ins[3].wait()
    ins[4].start()

    def cols(fb):
        return pl.ds(pl.multiple_of(fb * R, R), R)

    def gblock(fb):
        return lax.dot_general(tok[:, cols(fb)], s[...], (((0,), (0,)), ((), ())), preferred_element_type=F32)

    def send_g(d):
        gsend[d] = gblock(zto(d) * 2 + o).astype(BF16)
        c_g(d).start()

    def send_rp(d):
        mine = gblock(zto(d) * 2 + c)
        c_g(d).wait_recv()
        h[d] = (mine + grecv[d].astype(F32)).astype(BF16).reshape(h.shape[1:])
        if two_stage:
            c_r1(d, 1).start()
            c_r1(d, 0).start()
        else:
            for e in range(1, I):
                c_rp(e, d).start()

    send_g(0)

    def sketch(d, carry):
        send_g(d)
        send_rp(d - 1)
        return carry

    lax.fori_loop(1, Z, sketch, 0)
    send_rp(Z - 1)
    if cut:
        for d in range(1, Z):
            c_agd(d, f).start()

    acc[...] = jnp.zeros_like(acc)

    def c_tg(fb):
        return pltpu.make_async_copy(tg.at[fb], tg_h.at[:, cols(fb)], tg_sem.at[fb])

    def block(fb):
        wb = w[fb].reshape(R, KV)
        acc[...] += jnp.dot(tok[:, cols(fb)], wb, preferred_element_type=F32)
        product = lax.dot_general(up[...], wb, (((1,), (1,)), ((), ())), preferred_element_type=F32)
        tg[fb] = (product * inv_width).astype(BF16)
        c_tg(fb).start()

    def forward(d, carry):
        fb = zfrom(d) * 2 + c
        c_ag(d, fb, i).wait_recv()
        for e in range(1, I):
            @pl.when(ito(e) != far)
            def _():
                c_plane(e, d, fb, i).start()

        c_planed(d, fb, i).start()
        c_sib(0, d, fb, i).start()
        return carry

    if two_stage:
        lax.fori_loop(0, Z // 2, stage2, 0)
        lax.fori_loop(1, 2, forward, 0)
        lax.fori_loop(Z // 2, Z, stage2, 0)
        lax.fori_loop(2, Z, forward, 0)
    else:
        lax.fori_loop(1, Z, forward, 0)

    def send_rz(d, carry):
        total = h[d, i].astype(F32)
        if two_stage:
            c_r1(d, 0).wait_recv()
            c_r2(d).wait_recv()
            total += pb[1, d].astype(F32) + pb[3, d].astype(F32)
        else:
            for e in range(1, I):
                c_rp(e, d).wait_recv()
                total += pb[e, d].astype(F32)
        zb[d] = total.astype(BF16)

        @pl.when(d > 0)
        def _():
            c_rz(d).start()

        return carry

    lax.fori_loop(0, Z, send_rz, 0)

    factor = 1.0 / (math.sqrt(tok.shape[0] * 2 * Z) * projb.shape[1] * I)
    ins[4].wait()

    def out_np(part):
        return pltpu.make_async_copy(par.at[part], np_h.at[part], np_sem.at[part])

    def out_nm(part):
        return pltpu.make_async_copy(nm.at[part], nm_h.at[part], nm_sem.at[part])

    def finish(e, carry):
        part = ifrom(e)

        @pl.when(e > 0)
        def _():
            c_fin(e, part).wait_recv()

        outer = lax.dot_general(fin[part], projb[...], (((1,), (1,)), ((), ())), preferred_element_type=F32) * factor
        new_momentum = 0.9 * mom[part] + outer
        nm[part] = new_momentum
        par[part] = par[part] - 0.7 * (outer + 0.9 * new_momentum)
        out_np(part).start()
        out_nm(part).start()
        return carry

    def arrive(d):
        fb = zfrom(d) * 2 + c
        for e in range(1, I):
            @pl.when(ifrom(e) != far)
            def _():
                c_plane(e, d, fb, ifrom(e)).wait_recv()
                c_sib(e, d, fb, ifrom(e)).start()

        c_planed(d, fb, far).wait_recv()
        c_sibl(d, fb, far).start()

    def arrive_far(d):
        if cut:
            fb = zfrom(d) * 2 + c
            c_agd(d, fb).wait_recv()
            c_sibd(d, fb, far).start()

    def use(d):
        block(zfrom(d) * 2 + c)
        fo = zfrom(d) * 2 + o
        for e in range(I):
            @pl.when(ifrom(e) != far)
            def _():
                c_sib(e, d, fo, ifrom(e)).wait_recv()

        if cut:
            c_sibd(d, fo, far).wait_recv()
        c_sibl(d, fo, far).wait_recv()
        block(fo)

    block(f)
    c_own(z * 2 + o).wait_recv()
    block(z * 2 + o)

    arrive(1)

    total = zb[0].astype(F32)
    for d in range(1, Z):
        c_rz(d).wait_recv()
        total += zr[d].astype(F32)
    fin[i] = total.astype(BF16)
    for e in range(1, I):
        c_fin(e, i).start()

    def take(d, carry):
        arrive_far(d)
        arrive(d + 1)
        use(d)
        return carry

    lax.fori_loop(1, Z - 1, take, 0)
    arrive_far(Z - 1)
    lax.fori_loop(0, I, finish, 0)
    use(Z - 1)
    val[...] = (acc[...] * inv_width).astype(BF16)
    out_val = pltpu.make_async_copy(val, val_h, out_sem)
    out_val.start()

    def drain_z(d, carry):
        fb = zfrom(d) * 2 + c
        c_ag(d, f, i).wait_send()
        c_rz(d).wait_send()
        c_sib(0, d, fb, i).wait_send()
        for e in range(1, I):
            @pl.when(ito(e) != far)
            def _():
                c_plane(e, d, fb, i).wait_send()

            @pl.when(ifrom(e) != far)
            def _():
                c_sib(e, d, fb, ifrom(e)).wait_send()

        if cut:
            c_agd(d, f).wait_send()
            c_sibd(d, fb, far).wait_send()
        c_planed(d, fb, i).wait_send()
        c_sibl(d, fb, far).wait_send()
        return carry

    def drain_g(d, carry):
        c_g(d).wait_send()
        if two_stage:
            c_r1(d, 0).wait_send()
            c_r1(d, 1).wait_send()
            c_r2(d).wait_send()
        else:
            for e in range(1, I):
                c_rp(e, d).wait_send()
        return carry

    c_own(f).wait_send()
    lax.fori_loop(1, Z, drain_z, 0)
    lax.fori_loop(0, Z, drain_g, 0)
    for e in range(1, I):
        c_fin(e, i).wait_send()

    def drain_tg(k, carry):
        c_tg(k).wait()
        return carry

    lax.fori_loop(0, 2 * Z, drain_tg, 0)

    def drain_out(k, carry):
        out_np(k).wait()
        out_nm(k).wait()
        return carry

    lax.fori_loop(0, I, drain_out, 0)
    out_val.wait()


def local(Z, I, tokens, upstream, params, momentum, projection):
    T, D = tokens.shape
    R, KV = params.shape
    PR = projection.shape[1]
    q = R // I
    V = pltpu.VMEM
    dma = pltpu.SemaphoreType.DMA
    any_spec = pl.BlockSpec(memory_space=pl.ANY)
    outs = pl.pallas_call(
        functools.partial(kernel, Z, I),
        out_shape=(
            jax.ShapeDtypeStruct((T, KV), BF16),
            jax.ShapeDtypeStruct((T, D), BF16),
            jax.ShapeDtypeStruct((I, q, KV), F32),
            jax.ShapeDtypeStruct((I, q, KV), F32),
        ),
        in_specs=[pl.BlockSpec(memory_space=pltpu.HBM)] * 5,
        out_specs=(any_spec,) * 4,
        scratch_shapes=[
            V((T, D), BF16), V((T, KV), BF16), V((I, q, KV), F32), V((I, q, KV), F32), V((KV, PR), F32), V((KV, PR), BF16),
            V((2 * Z, I, q, KV), BF16), V((T, PR), BF16),
            V((Z, R, PR), BF16), V((Z, R, PR), BF16), V((Z, I, q, PR), BF16),
            V((I, Z, q, PR), BF16), V((Z, q, PR), BF16), V((Z, q, PR), BF16), V((I, q, PR), BF16),
            V((T, KV), F32), V((T, KV), BF16), V((2 * Z, T, R), BF16), V((I, q, KV), F32),
            dma((5,)), dma, dma((2 * Z,)), dma((I,)), dma((I,)),
            dma, dma, dma((Z,)), dma((Z,)), dma((I, Z)), dma((I, Z)), dma((I, Z)), dma((I, Z)),
            *[dma((Z,))] * 8,
            dma((Z,)), dma((Z,)), dma((I, Z)), dma((I, Z)), dma((Z,)), dma((Z,)), dma((I,)), dma((I,)),
        ],
        compiler_params=pltpu.CompilerParams(collective_id=0, has_side_effects=True, vmem_limit_bytes=46 * 2**20),
    )(tokens, upstream, params.reshape(I, q, KV), momentum.reshape(I, q, KV), projection)
    values, grads, new_params, new_momentum = outs
    return (values, grads, new_params.reshape(R, KV), new_momentum.reshape(R, KV))


def solution(mesh):
    I, F = mesh.shape["island"], mesh.shape["fsdp"]
    rows, shard, whole = P(("island", "fsdp"), None), P("fsdp", None), P()
    return jax.shard_map(
        functools.partial(local, F // 2, I), mesh=mesh,
        in_specs=(rows, rows, shard, shard, whole), out_specs=(rows, rows, shard, shard), check_vma=False,
    )
```
